32 devices in a mesh: clu: 8 (over z, x), grp: 4 (over y, core).
Axes of the slice: x: 2, y: 2, z: 4, core: 2. Of those that a mesh axis runs over, the one named last changes fastest.
Arguments:
- tokens: bfloat16 [32768, 1024], P(('clu', 'grp')), may hold values from -6 to 6
- segment_ids: int32 [32, 1024], P(('clu', 'grp')), may hold values from 0 to 127, never falling along the last dimension, each value on 1 to 32 neighbouring positions
- w_in: bfloat16 [1024, 2048], replicated, may hold values from -0.1875 to 0.1875
- b_in: float32 [2048], replicated, may hold values from -4 to 4
- w_out: bfloat16 [2048, 1024], replicated, may hold values from -0.125 to 0.125
- b_out: float32 [1024], replicated, may hold values from -1.5 to 1.5
- owner_ids: int32 [4096, 1], P(('clu', 'grp')), may hold values from 0 to 7; in each aligned block of 128 rows (0 to 127, 128 to 255, ...) at most 32 rows name the same one
- sub_ids: int32 [4096], P(('clu', 'grp')), may hold values from 0 to 255
Outputs:
- pooled: bfloat16 [4096, 1024], P(('clu', 'grp'))
- nearest: float32 [4096], P(('clu', 'grp'))
The draws below stay inside these ranges and needn't reach their ends.
Inputs may be any that keep to these rules, and one draw needn't show every extreme that they name: `owner_ids`: no device holds more than 32 documents of one owner; some device holds exactly 32. `segment_ids`: each row lists documents 0 to 127 in order, each on 1 to 32 consecutive positions, one on exactly 32.
All inputs are finite; a program needn't handle non-finite values.
Results may differ from the reference program's by a relative error of at most 0.0043.
Values may be sent and summed in bfloat16 or wider, within the bound.
A program may use at most 64 MiB of HBM per device.

```python
import math
import jax
import jax.numpy as jnp
import numpy as np
from jax import lax

D = 1024
FF = 2048
MOST_LEN = 32
TOK_DEV = 1024
DOCS_DEV = 128
SUBS = 256
CAP = 32
TOKENS = 32768
DOCS = 4096
N_CLU = 8
DEVICES = 32


def touch_ends(result, stream_key, low, largest):
    place = [jax.random.randint(jax.random.fold_in(stream_key, axis), (), 0, length) for axis, length in enumerate(result.shape)]
    widest = result.shape.index(max(result.shape))
    next_to = place[:widest] + [(place[widest] + 1) % result.shape[widest]] + place[widest + 1:]
    return result.at[tuple(place)].set(low).at[tuple(next_to)].set(largest)


def shard_levels(rng, extent, cuts, low, high):
    def one(axis_at, parts):
        steps = jax.random.uniform(jax.random.fold_in(jax.random.fold_in(rng, 6), axis_at), (parts,), jnp.float32, low / len(cuts), high / len(cuts))
        return jnp.repeat(jnp.exp(steps), extent[axis_at] // parts).reshape((-1,) + (1,) * (len(extent) - axis_at - 1))

    gain = one(*cuts[0])
    for cut in cuts[1:]:
        gain = gain * one(*cut)
    return gain


def length_profile(number_of, total, bound, lean):
    portions = [(1 << 20) // math.isqrt(standing ** lean) + 1 for standing in range(2, number_of + 1)]
    rest, holding = total - bound - (number_of - 1), [1] * (number_of - 1)
    while rest > 0:
        free = [i for i in range(number_of - 1) if holding[i] < bound]
        whole, budget = sum([portions[i] for i in free]), rest
        for i in free:
            addition = min(bound - holding[i], max(1, budget * portions[i] // whole), rest)
            holding[i] = holding[i] + addition
            rest = rest - addition
    return np.array([bound] + holding)


def ragged_sizes(stream_key, amount, total, most, slope):
    if amount == 2:
        one = jax.random.randint(stream_key, (), max(1, total - most), min(most, total - 1) + 1)
        return jnp.stack([one, total - one])
    lengths = jnp.asarray(length_profile(amount, total, most, slope), jnp.int32)
    couples = (amount - 1) // 2
    giver, sink = lengths[1:1 + 2 * couples:2], lengths[2:2 + 2 * couples:2]
    room = jnp.minimum(giver - 1, most - sink)
    shifted = jax.random.randint(jax.random.fold_in(stream_key, 1), (couples,), 0, 1 << 20) % (room + 1)
    lengths = lengths.at[1:1 + 2 * couples:2].set(giver - shifted).at[2:2 + 2 * couples:2].set(sink + shifted)
    return lengths[jax.random.permutation(jax.random.fold_in(stream_key, 2), amount)]


def assign_block(rng, own, number, rows, number_of, top, limit, skew):
    order = jax.random.permutation(rng, number_of)
    heavy_load, usual = shares(number_of, rows * top, limit, skew, True), shares(number_of, rows * top, limit, skew, False)
    places = jnp.arange(number_of)

    def named(lengths, offset_by):
        used = int((lengths > 0).sum())
        fixed = max(1, used // 4)
        shifted = fixed + (places - fixed + offset_by * (used - fixed)) % max(1, number_of - fixed)
        return jnp.zeros((number_of,), jnp.int32).at[order[jnp.where(places < fixed, places, shifted)]].set(jnp.asarray(lengths, jnp.int32))

    lengths = jnp.where(number % 4 == 0, named(heavy_load, number // 4), named(usual, number - number // 4 - 1))
    mixed = jax.random.permutation(jax.random.fold_in(own, 3), number_of)
    donor, receiver = mixed[0:number_of // 2 * 2:2], mixed[1:number_of // 2 * 2:2]
    slack = jnp.minimum(lengths[donor] - 1, limit - lengths[receiver]) // 2
    slack = jnp.where((donor == order[0]) | (receiver == order[0]) | (lengths[receiver] == 0), 0, jnp.maximum(slack, 0))
    shifted = jax.random.randint(jax.random.fold_in(own, 4), (number_of // 2,), 0, 1 << 20) % (slack + 1)
    lengths = lengths.at[donor].add(-shifted).at[receiver].add(shifted)
    labels = jnp.searchsorted(jnp.cumsum(lengths), jnp.arange(rows * top), side="right").astype(jnp.int32)
    grid = labels.reshape(top, rows).T
    grid = grid[jax.random.permutation(jax.random.fold_in(own, 1), rows)]
    offset_by = jax.random.randint(jax.random.fold_in(own, 2), (rows, 1), 0, top)
    return jnp.take_along_axis(grid, (jnp.arange(top)[None, :] + offset_by) % top, axis=1)


def shares(number_of, total, reach, slope, full):
    portions = [(1 << 20) // math.isqrt(grade ** slope) + 1 for grade in range(1, number_of + 1)]
    largest = reach if full else min(reach, max(-(-total // number_of), total * portions[0] // sum(portions)))
    least = 1 if total - largest >= number_of - 1 else 0
    given, spare = [largest] + [least] * (number_of - 1), total - largest - least * (number_of - 1)
    while spare > 0:
        movable = [i for i in range(1, number_of) if given[i] < largest] or [i for i in range(1, number_of) if given[i] < reach]
        mass, remaining = sum([portions[i] for i in movable]), spare
        for i in movable:
            extra = min(reach - given[i], max(1, remaining * portions[i] // mass), spare)
            given[i] = given[i] + extra
            spare = spare - extra
    return np.array(given)


def gaussian(key, shape, spread, most, pieces=(), held_as=jnp.bfloat16):
    entries = spread * jax.random.normal(key, shape, jnp.float32)
    if pieces:
        entries = entries * shard_levels(key, shape, pieces, -0.22, 0.18)
    return jnp.clip(entries, -most, most).astype(held_as)


def setup_inputs(seed: int = 0) -> dict:
    key_list = jax.random.split(jax.random.key(seed), 9)
    tokens = gaussian(key_list[0], (TOKENS, D), 1.0, 6.0, ((0, 32),))
    segment_ids = jax.vmap(lambda own: jnp.searchsorted(jnp.cumsum(ragged_sizes(own, DOCS_DEV, TOK_DEV, MOST_LEN, 2)), jnp.arange(TOK_DEV), side="right"))(jax.random.split(key_list[1], DEVICES)).reshape((DEVICES, TOK_DEV)).astype(jnp.int32)
    w_in = gaussian(key_list[2], (D, FF), D ** -0.5, 0.1875)
    b_in = gaussian(key_list[3], (FF,), 1.0, 4.0, (), jnp.float32)
    w_out = gaussian(key_list[4], (FF, D), FF ** -0.5, 0.125)
    b_out = gaussian(key_list[5], (D,), 0.3, 1.5, (), jnp.float32)
    owner_ids_keys = jax.random.split(jax.random.fold_in(key_list[6], 1), DOCS // DOCS_DEV)
    owner_ids_turns = jax.random.permutation(jax.random.fold_in(key_list[6], 3), DOCS // DOCS_DEV)
    owner_ids = jax.vmap(lambda own, number: assign_block(jax.random.fold_in(key_list[6], 2), own, number, DOCS_DEV, N_CLU, 1, CAP, 2))(owner_ids_keys, owner_ids_turns).reshape((DOCS, 1))
    sub_ids = touch_ends(jax.random.randint(key_list[7], (DOCS,), 0, SUBS), jax.random.fold_in(key_list[7], 1), 0, SUBS - 1).astype(jnp.int32)
    return dict(tokens=tokens, segment_ids=segment_ids, w_in=w_in, b_in=b_in, w_out=w_out, b_out=b_out, owner_ids=owner_ids, sub_ids=sub_ids)


def encode(token_block, segments, w_in, b_in, w_out, b_out, doc_count):
    pre_act = jnp.dot(token_block, w_in, preferred_element_type=jnp.float32) + b_in
    activated = jax.nn.gelu(pre_act, approximate=False).astype(jnp.bfloat16)
    layer_out = (token_block.astype(jnp.float32) + jnp.dot(activated, w_out, preferred_element_type=jnp.float32) + b_out).astype(jnp.bfloat16)
    member = segments[None, :] == jnp.arange(doc_count, dtype=jnp.int32)[:, None]
    totals = jnp.dot(member.astype(jnp.bfloat16), layer_out, preferred_element_type=jnp.float32)
    counts = lax.optimization_barrier(jnp.sum(member.astype(jnp.float32), axis=1, keepdims=True))
    mean_rows = totals / counts
    scale_inv = lax.rsqrt(lax.optimization_barrier(jnp.sum(mean_rows * mean_rows, axis=1, keepdims=True)) + 1e-06)
    return (mean_rows.astype(jnp.bfloat16), (mean_rows * scale_inv).astype(jnp.bfloat16))

def reference(tokens, segment_ids, w_in, b_in, w_out, b_out, owner_ids, sub_ids):
    blocks = tokens.reshape(DEVICES, TOK_DEV, D)

    def one_device(pair):
        return encode(pair[0], pair[1], w_in, b_in, w_out, b_out, DOCS_DEV)
    pooled, unit_rows = lax.map(one_device, (blocks, segment_ids))
    pooled = pooled.reshape(DOCS, D)
    unit_rows = unit_rows.reshape(DOCS, D)
    owner_rank = owner_ids[:, 0]
    row_limit = DEVICES * CAP

    def per_owner(owner_id):
        flags = jnp.where(owner_rank == owner_id, 0, 1).astype(jnp.int32)
        order_index = jnp.argsort(flags, stable=True)[:row_limit].astype(jnp.int32)
        valid_rows = owner_rank[order_index] == owner_id
        chosen = unit_rows[order_index]
        cluster_key = jnp.where(valid_rows, sub_ids[order_index], -1)
        similar = jnp.dot(chosen, chosen.T, preferred_element_type=jnp.float32)
        position = jnp.arange(row_limit, dtype=jnp.int32)
        matched = (cluster_key[:, None] == cluster_key[None, :]) & (cluster_key[:, None] >= 0) & (position[:, None] != position[None, :])
        best_sim = lax.optimization_barrier(jnp.max(jnp.where(matched, similar, -1.0), axis=1))
        return (order_index, jnp.where(valid_rows, best_sim, 0.0))
    orders, bests = lax.map(per_owner, jnp.arange(N_CLU, dtype=jnp.int32))
    nearest = jnp.zeros((DOCS,), jnp.float32).at[orders.reshape(-1)].add(bests.reshape(-1))
    return (pooled, nearest)
```

```python
import functools
import jax
import jax.numpy as jnp
from jax import lax
from jax.experimental import pallas as pl
from jax.experimental.pallas import tpu as pltpu
from jax.sharding import PartitionSpec as P

MESH = pl.DeviceIdType.MESH
F32 = jnp.float32
BF16 = jnp.bfloat16
META = 128
HI = 32
LO = 16


def gelu(x):
    return 0.5 * x * (1.0 + lax.erf(x * 0.7071067811865476))


def dot_nt(a, b):
    return lax.dot_general(a, b, (((1,), (1,)), ((), ())), preferred_element_type=F32)


def kernel(
    n_clu, n_grp, cap, parts,
    tok_hbm, seg_ref, w_in_hbm, b_in_ref, w_out_hbm, b_out_ref, owner_ref, sub_ref,
    pooled_ref, near_ref,
    tok, w_in, w_out, act, member, place, send, send_meta, gath, gath_meta, ret_out, ret_in,
    tok_sem, win_sem, wout_sem, a_send, a_recv, f_send, f_recv, r_send, r_recv,
):
    rows_n, width = tok.shape
    ff = w_in.shape[1]
    docs = pooled_ref.shape[0]
    slots = n_clu * cap
    col = width // parts
    n_y = n_grp // 2
    clu = lax.axis_index("clu")
    grp = lax.axis_index("grp")
    y_at, core = grp // 2, lax.rem(grp, 2)
    sib = y_at * 2 + 1 - core

    def peer(k):
        return lax.rem(clu + k, n_clu)

    def y_peer(t):
        return lax.rem(y_at + t, n_y) * 2 + core

    def y_source(t):
        return lax.rem(y_at + n_y - t, n_y) * 2 + core

    def y_source_sib(t):
        return lax.rem(y_at + n_y - t, n_y) * 2 + 1 - core

    f_parts = win_sem.shape[0]
    f_col = ff // f_parts

    def w_in_copy(f):
        at = pl.ds(pl.multiple_of(f * f_col, f_col), f_col)
        return pltpu.make_async_copy(w_in_hbm.at[:, at], w_in.at[:, at], win_sem.at[f])

    def w_out_copy(q):
        at = pl.ds(q * col, col)
        return pltpu.make_async_copy(w_out_hbm.at[:, at], w_out.at[:, at], wout_sem.at[q])

    tok_copy = pltpu.make_async_copy(tok_hbm, tok, tok_sem)
    tok_copy.start()
    for f in range(f_parts):
        w_in_copy(f).start()
    for q in range(parts):
        w_out_copy(q).start()

    barrier = pltpu.get_barrier_semaphore()
    for k in range(1, n_clu):
        pl.semaphore_signal(barrier, inc=1, device_id=(peer(k), grp), device_id_type=MESH)
    pl.semaphore_signal(barrier, inc=1, device_id=(clu, sib), device_id_type=MESH)
    for t in range(1, n_y):
        pl.semaphore_signal(barrier, inc=1, device_id=(clu, y_peer(t)), device_id_type=MESH)

    member[...] = (
        seg_ref[...] == lax.broadcasted_iota(jnp.int32, (docs, rows_n), 0)
    ).astype(F32).astype(BF16)
    sub = sub_ref[...]
    ones_at = lax.broadcasted_iota(jnp.int32, (docs, docs), 0) == lax.broadcasted_iota(
        jnp.int32, (docs, docs), 1
    )
    owner = jnp.sum(jnp.where(ones_at, owner_ref[...], 0), axis=0, keepdims=True)
    sub_col = jnp.sum(jnp.where(ones_at, sub, 0), axis=1, keepdims=True)
    hits = (lax.broadcasted_iota(jnp.int32, (n_clu, docs), 0) == owner).astype(F32)
    earlier = (
        lax.broadcasted_iota(jnp.int32, (docs, docs), 0)
        < lax.broadcasted_iota(jnp.int32, (docs, docs), 1)
    ).astype(F32).astype(BF16)
    before = jnp.dot(hits.astype(BF16), earlier, preferred_element_type=F32)
    slot = jnp.sum(before * hits, axis=0, keepdims=True).astype(jnp.int32)
    place[...] = (
        lax.broadcasted_iota(jnp.int32, (slots, docs), 0) == owner * cap + slot
    ).astype(F32).astype(BF16)
    lane = lax.broadcasted_iota(jnp.int32, (docs, META), 1)
    code = ((lane == sub_col // LO) | (lane == HI + lax.rem(sub_col, LO))).astype(F32)

    tok_copy.wait()
    blocks = 4
    block = rows_n // blocks

    @pl.loop(0, f_parts)
    def _(f):
        w_in_copy(f).wait()
        at = pl.ds(pl.multiple_of(f * f_col, f_col), f_col)
        bias = b_in_ref[:, at]

        def pre(r):
            return jnp.dot(
                tok[r * block:(r + 1) * block, :], w_in[:, at], preferred_element_type=F32
            )

        now = pre(0)
        for r in range(blocks):
            after = pre(r + 1) if r + 1 < blocks else None
            act[r * block:(r + 1) * block, at] = gelu(now + bias).astype(BF16)
            now = after

    def view(ref, part, g, at):
        return gath_meta.at[g, at] if part == parts else ref.at[g, part, at]

    def a_copy(part, k):
        source = send_meta if part == parts else send.at[part]
        return pltpu.make_async_remote_copy(
            src_ref=source.at[pl.ds(pl.multiple_of(peer(k) * cap, cap), cap)],
            dst_ref=view(gath, part, grp, pl.ds(pl.multiple_of(clu * cap, cap), cap)),
            send_sem=a_send.at[part, k], recv_sem=a_recv.at[part, k],
            device_id=(peer(k), grp), device_id_type=MESH,
        )

    every = pl.ds(0, slots)

    def f_copy(part, which, t):
        if which == "sib":
            g, to, s = grp, sib, 0
        elif which == "y":
            g, to, s = grp, y_peer(t), t
        else:
            g, to, s = y_source(t), sib, n_y - 1 + t
        return pltpu.make_async_remote_copy(
            src_ref=view(gath, part, g, every), dst_ref=view(gath, part, g, every),
            send_sem=f_send.at[part, s], recv_sem=f_recv.at[part, s],
            device_id=(clu, to), device_id_type=MESH,
        )

    def start_a(part, packed):
        source = send_meta if part == parts else send.at[part]
        source[...] = packed.astype(BF16)
        own = pl.ds(pl.multiple_of(clu * cap, cap), cap)
        mine = source[own, :]
        if part == parts:
            gath_meta[grp, own, :] = mine
        else:
            gath[grp, part, own, :] = mine
        for k in range(1, n_clu):
            a_copy(part, k).start()

    def turn(part):
        for k in range(1, n_clu):
            a_copy(part, k).wait_recv()
        for t in range(1, n_y):
            f_copy(part, "y", t).start()
        f_copy(part, "sib", 0).start()

    def pass_on(part):
        for t in range(1, n_y):
            f_copy(part, "y", t).wait_recv()
            f_copy(part, "on", t).start()

    counts = jnp.sum(member[...].astype(F32), axis=1, keepdims=True)
    squares = jnp.zeros((docs, 1), F32)
    for q in range(parts):
        w_out_copy(q).wait()
        at = slice(q * col, (q + 1) * col)
        totals = jnp.zeros((docs, col), F32)
        for r in range(blocks):
            rs = slice(r * block, (r + 1) * block)
            out = jnp.dot(act[rs, :], w_out[:, at], preferred_element_type=F32)
            out = (tok[rs, at].astype(F32) + out + b_out_ref[:, at]).astype(BF16)
            totals += jnp.dot(member[:, rs], out, preferred_element_type=F32)
        mean = totals / counts
        squares += jnp.sum(mean * mean, axis=1, keepdims=True)
        mean16 = mean.astype(BF16)
        pooled_ref[:, at] = mean16
        packed = jnp.dot(place[...], mean16, preferred_element_type=F32)
        if q == 0:
            pl.semaphore_wait(barrier, n_clu - 1 + n_y)
        start_a(q, packed)
        if q >= 2:
            turn(q - 2)
    inv = lax.rsqrt(squares + 1e-06)
    high = inv.astype(BF16).astype(F32)
    middle = (inv - high).astype(BF16).astype(F32)
    low = inv - high - middle
    norm_at = HI + LO
    meta = jnp.where(lane == norm_at, high, code)
    meta = jnp.where(lane == norm_at + 1, middle, meta)
    meta = jnp.where(lane == norm_at + 2, low, meta).astype(BF16)
    start_a(parts, jnp.dot(place[...], meta, preferred_element_type=F32))
    for part in range(max(0, parts - 2), parts + 1):
        turn(part)
    for part in range(parts + 1):
        pass_on(part)

    own_meta = gath_meta[grp]
    meta_lane = lax.broadcasted_iota(jnp.int32, (slots, META), 1)
    is_norm = (meta_lane >= norm_at) & (meta_lane < norm_at + 3)
    own_code = jnp.where(is_norm, 0.0, own_meta.astype(F32)).astype(BF16)
    pick_lane = lax.broadcasted_iota(jnp.int32, (8, META), 1)
    pick = ((pick_lane >= norm_at) & (pick_lane < norm_at + 3)).astype(F32).astype(BF16)
    own_inv = dot_nt(pick, own_meta)

    def best_of(g, itself):
        similar = jnp.zeros((slots, slots), F32)
        for q in range(parts):
            similar += dot_nt(gath[g, q], gath[grp, q])
        g_meta = gath_meta[g]
        inv_g = jnp.sum(jnp.where(is_norm, g_meta.astype(F32), 0.0), axis=1, keepdims=True)
        matched = dot_nt(g_meta, own_code) > 1.5
        if itself:
            matched = matched & (
                lax.broadcasted_iota(jnp.int32, (slots, slots), 0)
                != lax.broadcasted_iota(jnp.int32, (slots, slots), 1)
            )
        values = jnp.where(matched, similar * inv_g * own_inv[0:1, :], -1.0)
        return jnp.max(values, axis=0, keepdims=True)

    best = jnp.maximum(best_of(grp, True), -1.0)
    for part in range(parts + 1):
        f_copy(part, "sib", 0).wait_recv()
    best = jnp.maximum(best, best_of(sib, False))
    for t in range(1, n_y):
        best = jnp.maximum(best, best_of(y_source(t), False))
    for t in range(1, n_y):
        for part in range(parts + 1):
            f_copy(part, "on", t).wait_recv()
        best = jnp.maximum(best, best_of(y_source_sib(t), False))

    ret_out[...] = jnp.broadcast_to(best, (8, slots))
    ret_in[clu] = jnp.broadcast_to(best, (8, slots))

    def r_copy(k):
        return pltpu.make_async_remote_copy(
            src_ref=ret_out, dst_ref=ret_in.at[clu],
            send_sem=r_send.at[k], recv_sem=r_recv.at[k],
            device_id=(peer(k), grp), device_id_type=MESH,
        )

    for k in range(1, n_clu):
        r_copy(k).start()
    for part in range(parts + 1):
        for k in range(1, n_clu):
            a_copy(part, k).wait_send()
        f_copy(part, "sib", 0).wait_send()
        for t in range(1, n_y):
            f_copy(part, "y", t).wait_send()
            f_copy(part, "on", t).wait_send()
    for k in range(1, n_clu):
        r_copy(k).wait_recv()
    took = (
        lax.broadcasted_iota(jnp.int32, (slots, docs), 0) == clu * cap + slot
    ).astype(F32)
    got = jnp.concatenate([ret_in[c, 0:1, :] for c in range(n_clu)], axis=0)
    spread = jnp.dot(got, took, preferred_element_type=F32, precision=lax.Precision.HIGHEST)
    near_ref[...] = jnp.sum(spread * hits, axis=0, keepdims=True)
    for k in range(1, n_clu):
        r_copy(k).wait_send()


def per_device(tokens, segment_ids, w_in, b_in, w_out, b_out, owner_ids, sub_ids):
    n_clu = lax.axis_size("clu")
    n_grp = lax.axis_size("grp")
    docs = owner_ids.shape[0]
    rows_n, width = tokens.shape
    ff = w_in.shape[1]
    cap = max(16, 2 * docs // n_clu)
    slots = n_clu * cap
    parts = 4
    f_parts = 4
    n_y = n_grp // 2
    vmem = pl.BlockSpec(memory_space=pltpu.VMEM)
    hbm = pl.BlockSpec(memory_space=pl.ANY)
    dma = pltpu.SemaphoreType.DMA
    pooled, near = pl.pallas_call(
        functools.partial(kernel, n_clu, n_grp, cap, parts),
        out_shape=(
            jax.ShapeDtypeStruct((docs, width), BF16),
            jax.ShapeDtypeStruct((1, docs), F32),
        ),
        in_specs=[hbm, vmem, hbm, vmem, hbm, vmem, vmem, vmem],
        out_specs=(vmem, vmem),
        scratch_shapes=[
            pltpu.VMEM((rows_n, width), BF16),
            pltpu.VMEM((width, ff), BF16),
            pltpu.VMEM((ff, width), BF16),
            pltpu.VMEM((rows_n, ff), BF16),
            pltpu.VMEM((docs, rows_n), BF16),
            pltpu.VMEM((slots, docs), BF16),
            pltpu.VMEM((parts, slots, width // parts), BF16),
            pltpu.VMEM((slots, META), BF16),
            pltpu.VMEM((n_grp, parts, slots, width // parts), BF16),
            pltpu.VMEM((n_grp, slots, META), BF16),
            pltpu.VMEM((8, slots), F32),
            pltpu.VMEM((n_clu, 8, slots), F32),
            dma(()),
            dma((f_parts,)),
            dma((parts,)),
            dma((parts + 1, n_clu)),
            dma((parts + 1, n_clu)),
            dma((parts + 1, 2 * n_y)),
            dma((parts + 1, 2 * n_y)),
            dma((n_clu,)),
            dma((n_clu,)),
        ],
        compiler_params=pltpu.CompilerParams(
            collective_id=0, has_side_effects=True, vmem_limit_bytes=56 * 1024 * 1024
        ),
    )(
        tokens, segment_ids, w_in, b_in.reshape(1, ff), w_out, b_out.reshape(1, width),
        owner_ids, sub_ids.reshape(1, docs),
    )
    return (pooled, near.reshape(docs))


def solution(mesh):
    in_specs = (
        P(("clu", "grp"), None),
        P(("clu", "grp"), None),
        P(),
        P(),
        P(),
        P(),
        P(("clu", "grp"), None),
        P(("clu", "grp")),
    )
    out_specs = (P(("clu", "grp"), None), P(("clu", "grp")))
    return jax.shard_map(
        per_device, mesh=mesh, in_specs=in_specs, out_specs=out_specs, check_vma=False
    )
```

```python
import functools
import jax
import jax.numpy as jnp
from jax import lax
from jax.experimental import pallas as pl
from jax.experimental.pallas import tpu as pltpu
from jax.sharding import PartitionSpec as P

MESH = pl.DeviceIdType.MESH
F32 = jnp.float32
BF16 = jnp.bfloat16
META = 128
HI = 32
LO = 16


def gelu(x):
    size = jnp.abs(x)
    t = 1.0 / (1.0 + 0.23164190091 * size)
    tail = 0.5307027145
    for term in (-0.7265760135, 0.7107068705, -0.142248368, 0.127414796):
        tail = tail * t + term
    tail = tail * t * size * jnp.exp2(x * x * -0.72134752044448)
    return jnp.maximum(x, 0.0) - tail


def dot_nt(a, b):
    return lax.dot_general(a, b, (((1,), (1,)), ((), ())), preferred_element_type=F32)


def kernel(
    n_clu, n_grp, cap, parts,
    tok_hbm, seg_ref, w_in_hbm, b_in_ref, w_out_hbm, b_out_ref, owner_ref, sub_ref,
    pooled_ref, near_ref,
    tok, w_in, w_out, act, member, place, send, send_meta, gath, gath_meta, ret_out, ret_in,
    tok_sem, win_sem, wout_sem, a_send, a_recv, f_send, f_recv, r_send, r_recv,
):
    rows_n, width = tok.shape
    ff = w_in.shape[1]
    docs = pooled_ref.shape[0]
    slots = n_clu * cap
    col = width // parts
    n_y = n_grp // 2
    clu = lax.axis_index("clu")
    grp = lax.axis_index("grp")
    y_at, core = grp // 2, lax.rem(grp, 2)
    sib = y_at * 2 + 1 - core

    def peer(k):
        return lax.rem(clu + k, n_clu)

    def y_peer(t):
        return lax.rem(y_at + t, n_y) * 2 + core

    def y_source(t):
        return lax.rem(y_at + n_y - t, n_y) * 2 + core

    def y_source_sib(t):
        return lax.rem(y_at + n_y - t, n_y) * 2 + 1 - core

    f_parts = win_sem.shape[0]
    f_col = ff // f_parts

    def w_in_copy(f):
        at = pl.ds(pl.multiple_of(f * f_col, f_col), f_col)
        return pltpu.make_async_copy(w_in_hbm.at[:, at], w_in.at[:, at], win_sem.at[f])

    def w_out_copy(q):
        at = pl.ds(q * col, col)
        return pltpu.make_async_copy(w_out_hbm.at[:, at], w_out.at[:, at], wout_sem.at[q])

    tok_copy = pltpu.make_async_copy(tok_hbm, tok, tok_sem)
    tok_copy.start()
    for f in range(f_parts):
        w_in_copy(f).start()
    for q in range(parts):
        w_out_copy(q).start()

    barrier = pltpu.get_barrier_semaphore()
    for k in range(1, n_clu):
        pl.semaphore_signal(barrier, inc=1, device_id=(peer(k), grp), device_id_type=MESH)
    pl.semaphore_signal(barrier, inc=1, device_id=(clu, sib), device_id_type=MESH)
    for t in range(1, n_y):
        pl.semaphore_signal(barrier, inc=1, device_id=(clu, y_peer(t)), device_id_type=MESH)

    member[...] = (
        seg_ref[...] == lax.broadcasted_iota(jnp.int32, (docs, rows_n), 0)
    ).astype(F32).astype(BF16)
    sub = sub_ref[...]
    ones_at = lax.broadcasted_iota(jnp.int32, (docs, docs), 0) == lax.broadcasted_iota(
        jnp.int32, (docs, docs), 1
    )
    owner = owner_ref[...]
    sub_col = jnp.sum(jnp.where(ones_at, sub, 0), axis=1, keepdims=True)
    hits = (lax.broadcasted_iota(jnp.int32, (n_clu, docs), 0) == owner).astype(F32)
    earlier = (
        lax.broadcasted_iota(jnp.int32, (docs, docs), 0)
        < lax.broadcasted_iota(jnp.int32, (docs, docs), 1)
    ).astype(F32).astype(BF16)
    before = jnp.dot(hits.astype(BF16), earlier, preferred_element_type=F32)
    slot = jnp.sum(before * hits, axis=0, keepdims=True).astype(jnp.int32)
    place[...] = (
        lax.broadcasted_iota(jnp.int32, (slots, docs), 0) == owner * cap + slot
    ).astype(F32).astype(BF16)
    lane = lax.broadcasted_iota(jnp.int32, (docs, META), 1)
    code = ((lane == sub_col // LO) | (lane == HI + lax.rem(sub_col, LO))).astype(F32).astype(BF16)

    def view(ref, part, g, at):
        return gath_meta.at[g, at] if part == parts else ref.at[g, part, at]

    def a_copy(part, k):
        source = send_meta if part == parts else send.at[part]
        return pltpu.make_async_remote_copy(
            src_ref=source.at[pl.ds(pl.multiple_of(peer(k) * cap, cap), cap)],
            dst_ref=view(gath, part, grp, pl.ds(pl.multiple_of(clu * cap, cap), cap)),
            send_sem=a_send.at[part, k], recv_sem=a_recv.at[part, k],
            device_id=(peer(k), grp), device_id_type=MESH,
        )

    every = pl.ds(0, slots)

    def f_copy(part, which, t):
        if which == "sib":
            g, to, s = grp, sib, 0
        elif which == "y":
            g, to, s = grp, y_peer(t), t
        else:
            g, to, s = y_source(t), sib, n_y - 1 + t
        return pltpu.make_async_remote_copy(
            src_ref=view(gath, part, g, every), dst_ref=view(gath, part, g, every),
            send_sem=f_send.at[part, s], recv_sem=f_recv.at[part, s],
            device_id=(clu, to), device_id_type=MESH,
        )

    def start_a(part, packed):
        source = send_meta if part == parts else send.at[part]
        source[...] = packed.astype(BF16)
        own = pl.ds(pl.multiple_of(clu * cap, cap), cap)
        mine = source[own, :]
        if part == parts:
            gath_meta[grp, own, :] = mine
        else:
            gath[grp, part, own, :] = mine
        for k in range(1, n_clu):
            a_copy(part, k).start()

    def turn(part):
        for k in range(1, n_clu):
            a_copy(part, k).wait_recv()
        for t in range(1, n_y):
            f_copy(part, "y", t).start()
        f_copy(part, "sib", 0).start()

    def pass_on(part):
        for t in range(1, n_y):
            f_copy(part, "y", t).wait_recv()
            f_copy(part, "on", t).start()
    pl.semaphore_wait(barrier, n_clu - 1 + n_y)
    start_a(parts, jnp.dot(place[...], code, preferred_element_type=F32))

    tok_copy.wait()
    blocks = 4
    block = rows_n // blocks

    @pl.loop(0, f_parts)
    def _(f):
        w_in_copy(f).wait()
        at = pl.ds(pl.multiple_of(f * f_col, f_col), f_col)
        bias = b_in_ref[:, at]

        def pre(r):
            return jnp.dot(
                tok[r * block:(r + 1) * block, :], w_in[:, at], preferred_element_type=F32
            )

        now = pre(0)
        for r in range(blocks):
            after = pre(r + 1) if r + 1 < blocks else None
            act[r * block:(r + 1) * block, at] = gelu(now + bias).astype(BF16)
            now = after

    turn(parts)
    counts = jnp.sum(member[...].astype(F32), axis=1, keepdims=True)
    for q in range(parts):
        w_out_copy(q).wait()
        at = slice(q * col, (q + 1) * col)
        totals = jnp.zeros((docs, col), F32)
        for r in range(blocks):
            rs = slice(r * block, (r + 1) * block)
            out = jnp.dot(act[rs, :], w_out[:, at], preferred_element_type=F32)
            out = (tok[rs, at].astype(F32) + out + b_out_ref[:, at]).astype(BF16)
            totals += jnp.dot(member[:, rs], out, preferred_element_type=F32)
        mean = totals / counts
        mean16 = mean.astype(BF16)
        pooled_ref[:, at] = mean16
        packed = jnp.dot(place[...], mean16, preferred_element_type=F32)
        start_a(q, packed)
        if q == 0:
            pass_on(parts)
        if q >= 2:
            turn(q - 2)
    for part in range(max(0, parts - 2), parts):
        turn(part)
    for part in range(parts - 1):
        pass_on(part)

    own_code = gath_meta[grp]
    diagonal = lax.broadcasted_iota(jnp.int32, (slots, slots), 0) == lax.broadcasted_iota(
        jnp.int32, (slots, slots), 1
    )

    def products(g):
        similar = jnp.zeros((slots, slots), F32)
        for q in range(parts):
            similar += dot_nt(gath[g, q], gath[grp, q])
        return similar

    def inverse(squares):
        return lax.rsqrt(squares + 1e-06)

    def matches(g):
        return dot_nt(gath_meta[g], own_code) > 1.5

    similar = products(grp)
    own_squares = jnp.where(diagonal, similar, 0.0)
    across = inverse(jnp.sum(own_squares, axis=0, keepdims=True))
    down = inverse(jnp.sum(own_squares, axis=1, keepdims=True))
    values = jnp.where(matches(grp) & ~diagonal, similar * down * across, -1.0)
    best = jnp.maximum(jnp.max(values, axis=0, keepdims=True), -1.0)

    def best_of(g):
        squares = jnp.zeros((slots, 1), F32)
        for q in range(parts):
            rows = gath[g, q].astype(F32)
            squares += jnp.sum(rows * rows, axis=1, keepdims=True)
        values = jnp.where(matches(g), products(g) * inverse(squares) * across, -1.0)
        return jnp.max(values, axis=0, keepdims=True)

    for part in range(parts + 1):
        f_copy(part, "sib", 0).wait_recv()
    best = jnp.maximum(best, best_of(sib))
    pass_on(parts - 1)
    for t in range(1, n_y):
        best = jnp.maximum(best, best_of(y_source(t)))
    for t in range(1, n_y):
        for part in range(parts + 1):
            f_copy(part, "on", t).wait_recv()
        best = jnp.maximum(best, best_of(y_source_sib(t)))

    ret_out[...] = jnp.broadcast_to(best, (8, slots))
    ret_in[clu] = jnp.broadcast_to(best, (8, slots))

    def r_copy(k):
        return pltpu.make_async_remote_copy(
            src_ref=ret_out, dst_ref=ret_in.at[clu],
            send_sem=r_send.at[k], recv_sem=r_recv.at[k],
            device_id=(peer(k), grp), device_id_type=MESH,
        )

    for k in range(1, n_clu):
        r_copy(k).start()
    for part in range(parts + 1):
        for k in range(1, n_clu):
            a_copy(part, k).wait_send()
        f_copy(part, "sib", 0).wait_send()
        for t in range(1, n_y):
            f_copy(part, "y", t).wait_send()
            f_copy(part, "on", t).wait_send()
    for k in range(1, n_clu):
        r_copy(k).wait_recv()
    took = (
        lax.broadcasted_iota(jnp.int32, (slots, docs), 0) == clu * cap + slot
    ).astype(F32)
    got = jnp.concatenate([ret_in[c, 0:1, :] for c in range(n_clu)], axis=0)
    spread = jnp.dot(got, took, preferred_element_type=F32, precision=lax.Precision.HIGHEST)
    near_ref[...] = jnp.sum(spread * hits, axis=0, keepdims=True)
    for k in range(1, n_clu):
        r_copy(k).wait_send()


def per_device(tokens, segment_ids, w_in, b_in, w_out, b_out, owner_ids, sub_ids):
    n_clu = lax.axis_size("clu")
    n_grp = lax.axis_size("grp")
    docs = owner_ids.shape[0]
    rows_n, width = tokens.shape
    ff = w_in.shape[1]
    cap = max(16, 2 * docs // n_clu)
    slots = n_clu * cap
    parts = 4
    f_parts = 4
    n_y = n_grp // 2
    vmem = pl.BlockSpec(memory_space=pltpu.VMEM)
    hbm = pl.BlockSpec(memory_space=pl.ANY)
    dma = pltpu.SemaphoreType.DMA
    pooled, near = pl.pallas_call(
        functools.partial(kernel, n_clu, n_grp, cap, parts),
        out_shape=(
            jax.ShapeDtypeStruct((docs, width), BF16),
            jax.ShapeDtypeStruct((1, docs), F32),
        ),
        in_specs=[hbm, vmem, hbm, vmem, hbm, vmem, vmem, vmem],
        out_specs=(vmem, vmem),
        scratch_shapes=[
            pltpu.VMEM((rows_n, width), BF16),
            pltpu.VMEM((width, ff), BF16),
            pltpu.VMEM((ff, width), BF16),
            pltpu.VMEM((rows_n, ff), BF16),
            pltpu.VMEM((docs, rows_n), BF16),
            pltpu.VMEM((slots, docs), BF16),
            pltpu.VMEM((parts, slots, width // parts), BF16),
            pltpu.VMEM((slots, META), BF16),
            pltpu.VMEM((n_grp, parts, slots, width // parts), BF16),
            pltpu.VMEM((n_grp, slots, META), BF16),
            pltpu.VMEM((8, slots), F32),
            pltpu.VMEM((n_clu, 8, slots), F32),
            dma(()),
            dma((f_parts,)),
            dma((parts,)),
            dma((parts + 1, n_clu)),
            dma((parts + 1, n_clu)),
            dma((parts + 1, 2 * n_y)),
            dma((parts + 1, 2 * n_y)),
            dma((n_clu,)),
            dma((n_clu,)),
        ],
        compiler_params=pltpu.CompilerParams(
            collective_id=0, has_side_effects=True, vmem_limit_bytes=56 * 1024 * 1024
        ),
    )(
        tokens, segment_ids, w_in, b_in.reshape(1, ff), w_out, b_out.reshape(1, width),
        owner_ids.reshape(1, docs), sub_ids.reshape(1, docs),
    )
    return (pooled, near.reshape(docs))


def solution(mesh):
    in_specs = (
        P(("clu", "grp"), None),
        P(("clu", "grp"), None),
        P(),
        P(),
        P(),
        P(),
        P(("clu", "grp"), None),
        P(("clu", "grp")),
    )
    out_specs = (P(("clu", "grp"), None), P(("clu", "grp")))
    return jax.shard_map(
        per_device, mesh=mesh, in_specs=in_specs, out_specs=out_specs, check_vma=False
    )
```

```python
import functools
import jax
import jax.numpy as jnp
from jax import lax
from jax.experimental import pallas as pl
from jax.experimental.pallas import tpu as pltpu
from jax.sharding import PartitionSpec as P

MESH = pl.DeviceIdType.MESH
F32 = jnp.float32
BF16 = jnp.bfloat16
META = 128
HI = 32
LO = 16


def gelu(x):
    return 0.5 * x * (1.0 + lax.erf(x * 0.7071067811865476))


def dot_nt(a, b):
    return lax.dot_general(a, b, (((1,), (1,)), ((), ())), preferred_element_type=F32)


def kernel(
    n_clu, n_grp, cap, parts,
    tok_hbm, seg_ref, w_in_hbm, b_in_ref, w_out_hbm, b_out_ref, owner_ref, sub_ref,
    pooled_ref, near_ref,
    tok, w_in, w_out, act, member, place, send, send_meta, gath, gath_meta, ret_out, ret_in,
    tok_sem, win_sem, wout_sem, a_send, a_recv, f_send, f_recv, r_send, r_recv,
):
    rows_n, width = tok.shape
    ff = w_in.shape[1]
    docs = pooled_ref.shape[0]
    slots = n_clu * cap
    col = width // parts
    n_y = n_grp // 2
    clu = lax.axis_index("clu")
    grp = lax.axis_index("grp")
    y_at, core = grp // 2, lax.rem(grp, 2)
    sib = y_at * 2 + 1 - core

    def peer(k):
        return lax.rem(clu + k, n_clu)

    def y_peer(t):
        return lax.rem(y_at + t, n_y) * 2 + core

    def y_source(t):
        return lax.rem(y_at + n_y - t, n_y) * 2 + core

    def y_source_sib(t):
        return lax.rem(y_at + n_y - t, n_y) * 2 + 1 - core

    f_parts = win_sem.shape[0]
    f_col = ff // f_parts

    def w_in_copy(f):
        at = pl.ds(pl.multiple_of(f * f_col, f_col), f_col)
        return pltpu.make_async_copy(w_in_hbm.at[:, at], w_in.at[:, at], win_sem.at[f])

    def w_out_copy(q):
        at = pl.ds(q * col, col)
        return pltpu.make_async_copy(w_out_hbm.at[:, at], w_out.at[:, at], wout_sem.at[q])

    tok_copy = pltpu.make_async_copy(tok_hbm, tok, tok_sem)
    tok_copy.start()
    for f in range(f_parts):
        w_in_copy(f).start()
    for q in range(parts):
        w_out_copy(q).start()

    barrier = pltpu.get_barrier_semaphore()
    for k in range(1, n_clu):
        pl.semaphore_signal(barrier, inc=1, device_id=(peer(k), grp), device_id_type=MESH)
    pl.semaphore_signal(barrier, inc=1, device_id=(clu, sib), device_id_type=MESH)
    for t in range(1, n_y):
        pl.semaphore_signal(barrier, inc=1, device_id=(clu, y_peer(t)), device_id_type=MESH)

    member[...] = (
        seg_ref[...] == lax.broadcasted_iota(jnp.int32, (docs, rows_n), 0)
    ).astype(F32).astype(BF16)
    sub = sub_ref[...]
    ones_at = lax.broadcasted_iota(jnp.int32, (docs, docs), 0) == lax.broadcasted_iota(
        jnp.int32, (docs, docs), 1
    )
    owner = owner_ref[...]
    sub_col = jnp.sum(jnp.where(ones_at, sub, 0), axis=1, keepdims=True)
    hits = (lax.broadcasted_iota(jnp.int32, (n_clu, docs), 0) == owner).astype(F32)
    earlier = (
        lax.broadcasted_iota(jnp.int32, (docs, docs), 0)
        < lax.broadcasted_iota(jnp.int32, (docs, docs), 1)
    ).astype(F32).astype(BF16)
    before = jnp.dot(hits.astype(BF16), earlier, preferred_element_type=F32)
    slot = jnp.sum(before * hits, axis=0, keepdims=True).astype(jnp.int32)
    place[...] = (
        lax.broadcasted_iota(jnp.int32, (slots, docs), 0) == owner * cap + slot
    ).astype(F32).astype(BF16)
    lane = lax.broadcasted_iota(jnp.int32, (docs, META), 1)
    code = ((lane == sub_col // LO) | (lane == HI + lax.rem(sub_col, LO))).astype(F32)

    tok_copy.wait()
    blocks = 4
    block = rows_n // blocks

    @pl.loop(0, f_parts)
    def _(f):
        w_in_copy(f).wait()
        at = pl.ds(pl.multiple_of(f * f_col, f_col), f_col)
        bias = b_in_ref[:, at]

        def pre(r):
            return jnp.dot(
                tok[r * block:(r + 1) * block, :], w_in[:, at], preferred_element_type=F32
            )

        now = pre(0)
        for r in range(blocks):
            after = pre(r + 1) if r + 1 < blocks else None
            act[r * block:(r + 1) * block, at] = gelu(now + bias).astype(BF16)
            now = after

    def view(ref, part, g, at):
        return gath_meta.at[g, at] if part == parts else ref.at[g, part, at]

    def a_copy(part, k):
        source = send_meta if part == parts else send.at[part]
        return pltpu.make_async_remote_copy(
            src_ref=source.at[pl.ds(pl.multiple_of(peer(k) * cap, cap), cap)],
            dst_ref=view(gath, part, grp, pl.ds(pl.multiple_of(clu * cap, cap), cap)),
            send_sem=a_send.at[part, k], recv_sem=a_recv.at[part, k],
            device_id=(peer(k), grp), device_id_type=MESH,
        )

    every = pl.ds(0, slots)

    def f_copy(part, which, t):
        if which == "sib":
            g, to, s = grp, sib, 0
        elif which == "y":
            g, to, s = grp, y_peer(t), t
        else:
            g, to, s = y_source(t), sib, n_y - 1 + t
        return pltpu.make_async_remote_copy(
            src_ref=view(gath, part, g, every), dst_ref=view(gath, part, g, every),
            send_sem=f_send.at[part, s], recv_sem=f_recv.at[part, s],
            device_id=(clu, to), device_id_type=MESH,
        )

    def start_a(part, packed):
        source = send_meta if part == parts else send.at[part]
        source[...] = packed.astype(BF16)
        own = pl.ds(pl.multiple_of(clu * cap, cap), cap)
        mine = source[own, :]
        if part == parts:
            gath_meta[grp, own, :] = mine
        else:
            gath[grp, part, own, :] = mine
        for k in range(1, n_clu):
            a_copy(part, k).start()

    def turn(part):
        for k in range(1, n_clu):
            a_copy(part, k).wait_recv()
        for t in range(1, n_y):
            f_copy(part, "y", t).start()
        f_copy(part, "sib", 0).start()

    def pass_on(part):
        for t in range(1, n_y):
            f_copy(part, "y", t).wait_recv()
            f_copy(part, "on", t).start()

    counts = jnp.sum(member[...].astype(F32), axis=1, keepdims=True)
    squares = jnp.zeros((docs, 1), F32)
    for q in range(parts):
        w_out_copy(q).wait()
        at = slice(q * col, (q + 1) * col)
        totals = jnp.zeros((docs, col), F32)
        for r in range(blocks):
            rs = slice(r * block, (r + 1) * block)
            out = jnp.dot(act[rs, :], w_out[:, at], preferred_element_type=F32)
            out = (tok[rs, at].astype(F32) + out + b_out_ref[:, at]).astype(BF16)
            totals += jnp.dot(member[:, rs], out, preferred_element_type=F32)
        mean = totals / counts
        squares += jnp.sum(mean * mean, axis=1, keepdims=True)
        mean16 = mean.astype(BF16)
        pooled_ref[:, at] = mean16
        packed = jnp.dot(place[...], mean16, preferred_element_type=F32)
        if q == 0:
            pl.semaphore_wait(barrier, n_clu - 1 + n_y)
        start_a(q, packed)
        if q >= 2:
            turn(q - 2)
    inv = lax.rsqrt(squares + 1e-06)
    high = inv.astype(BF16).astype(F32)
    middle = (inv - high).astype(BF16).astype(F32)
    low = inv - high - middle
    norm_at = HI + LO
    meta = jnp.where(lane == norm_at, high, code)
    meta = jnp.where(lane == norm_at + 1, middle, meta)
    meta = jnp.where(lane == norm_at + 2, low, meta).astype(BF16)
    start_a(parts, jnp.dot(place[...], meta, preferred_element_type=F32))
    for part in range(max(0, parts - 2), parts + 1):
        turn(part)
    for part in range(parts - 1):
        pass_on(part)

    own_meta = gath_meta[grp]
    meta_lane = lax.broadcasted_iota(jnp.int32, (slots, META), 1)
    is_norm = (meta_lane >= norm_at) & (meta_lane < norm_at + 3)
    own_code = jnp.where(is_norm, 0.0, own_meta.astype(F32)).astype(BF16)
    pick_lane = lax.broadcasted_iota(jnp.int32, (8, META), 1)
    pick = ((pick_lane >= norm_at) & (pick_lane < norm_at + 3)).astype(F32).astype(BF16)
    own_inv = dot_nt(pick, own_meta)

    def best_of(g, itself):
        similar = jnp.zeros((slots, slots), F32)
        for q in range(parts):
            similar += dot_nt(gath[g, q], gath[grp, q])
        g_meta = gath_meta[g]
        inv_g = jnp.sum(jnp.where(is_norm, g_meta.astype(F32), 0.0), axis=1, keepdims=True)
        matched = dot_nt(g_meta, own_code) > 1.5
        if itself:
            matched = matched & (
                lax.broadcasted_iota(jnp.int32, (slots, slots), 0)
                != lax.broadcasted_iota(jnp.int32, (slots, slots), 1)
            )
        values = jnp.where(matched, similar * inv_g * own_inv[0:1, :], -1.0)
        return jnp.max(values, axis=0, keepdims=True)

    best = jnp.maximum(best_of(grp, True), -1.0)
    for part in range(parts + 1):
        f_copy(part, "sib", 0).wait_recv()
    best = jnp.maximum(best, best_of(sib, False))
    for part in range(parts - 1, parts + 1):
        pass_on(part)
    for t in range(1, n_y):
        best = jnp.maximum(best, best_of(y_source(t), False))
    for t in range(1, n_y):
        for part in range(parts + 1):
            f_copy(part, "on", t).wait_recv()
        best = jnp.maximum(best, best_of(y_source_sib(t), False))

    ret_out[...] = jnp.broadcast_to(best, (8, slots))
    ret_in[clu] = jnp.broadcast_to(best, (8, slots))

    def r_copy(k):
        return pltpu.make_async_remote_copy(
            src_ref=ret_out, dst_ref=ret_in.at[clu],
            send_sem=r_send.at[k], recv_sem=r_recv.at[k],
            device_id=(peer(k), grp), device_id_type=MESH,
        )

    for k in range(1, n_clu):
        r_copy(k).start()
    for part in range(parts + 1):
        for k in range(1, n_clu):
            a_copy(part, k).wait_send()
        f_copy(part, "sib", 0).wait_send()
        for t in range(1, n_y):
            f_copy(part, "y", t).wait_send()
            f_copy(part, "on", t).wait_send()
    for k in range(1, n_clu):
        r_copy(k).wait_recv()
    took = (
        lax.broadcasted_iota(jnp.int32, (slots, docs), 0) == clu * cap + slot
    ).astype(F32)
    got = jnp.concatenate([ret_in[c, 0:1, :] for c in range(n_clu)], axis=0)
    spread = jnp.dot(got, took, preferred_element_type=F32, precision=lax.Precision.HIGHEST)
    near_ref[...] = jnp.sum(spread * hits, axis=0, keepdims=True)
    for k in range(1, n_clu):
        r_copy(k).wait_send()


def per_device(tokens, segment_ids, w_in, b_in, w_out, b_out, owner_ids, sub_ids):
    n_clu = lax.axis_size("clu")
    n_grp = lax.axis_size("grp")
    docs = owner_ids.shape[0]
    rows_n, width = tokens.shape
    ff = w_in.shape[1]
    cap = max(16, 2 * docs // n_clu)
    slots = n_clu * cap
    parts = 4
    f_parts = 4
    n_y = n_grp // 2
    vmem = pl.BlockSpec(memory_space=pltpu.VMEM)
    hbm = pl.BlockSpec(memory_space=pl.ANY)
    dma = pltpu.SemaphoreType.DMA
    pooled, near = pl.pallas_call(
        functools.partial(kernel, n_clu, n_grp, cap, parts),
        out_shape=(
            jax.ShapeDtypeStruct((docs, width), BF16),
            jax.ShapeDtypeStruct((1, docs), F32),
        ),
        in_specs=[hbm, vmem, hbm, vmem, hbm, vmem, vmem, vmem],
        out_specs=(vmem, vmem),
        scratch_shapes=[
            pltpu.VMEM((rows_n, width), BF16),
            pltpu.VMEM((width, ff), BF16),
            pltpu.VMEM((ff, width), BF16),
            pltpu.VMEM((rows_n, ff), BF16),
            pltpu.VMEM((docs, rows_n), BF16),
            pltpu.VMEM((slots, docs), BF16),
            pltpu.VMEM((parts, slots, width // parts), BF16),
            pltpu.VMEM((slots, META), BF16),
            pltpu.VMEM((n_grp, parts, slots, width // parts), BF16),
            pltpu.VMEM((n_grp, slots, META), BF16),
            pltpu.VMEM((8, slots), F32),
            pltpu.VMEM((n_clu, 8, slots), F32),
            dma(()),
            dma((f_parts,)),
            dma((parts,)),
            dma((parts + 1, n_clu)),
            dma((parts + 1, n_clu)),
            dma((parts + 1, 2 * n_y)),
            dma((parts + 1, 2 * n_y)),
            dma((n_clu,)),
            dma((n_clu,)),
        ],
        compiler_params=pltpu.CompilerParams(
            collective_id=0, has_side_effects=True, vmem_limit_bytes=56 * 1024 * 1024
        ),
    )(
        tokens, segment_ids, w_in, b_in.reshape(1, ff), w_out, b_out.reshape(1, width),
        owner_ids.reshape(1, docs), sub_ids.reshape(1, docs),
    )
    return (pooled, near.reshape(docs))


def solution(mesh):
    in_specs = (
        P(("clu", "grp"), None),
        P(("clu", "grp"), None),
        P(),
        P(),
        P(),
        P(),
        P(("clu", "grp"), None),
        P(("clu", "grp")),
    )
    out_specs = (P(("clu", "grp"), None), P(("clu", "grp")))
    return jax.shard_map(
        per_device, mesh=mesh, in_specs=in_specs, out_specs=out_specs, check_vma=False
    )
```

```python
import functools
import jax
import jax.numpy as jnp
from jax import lax
from jax.experimental import pallas as pl
from jax.experimental.pallas import tpu as pltpu
from jax.sharding import PartitionSpec as P

MESH = pl.DeviceIdType.MESH
F32 = jnp.float32
BF16 = jnp.bfloat16
META = 128
HI = 32
LO = 16


def gelu(x):
    size = jnp.abs(x)
    below = 1.0 + 0.23164190091 * size
    t = pl.reciprocal(below, approx=True)
    t = t * (2.0 - below * t)
    tail = 0.5307027145
    for term in (-0.7265760135, 0.7107068705, -0.142248368, 0.127414796):
        tail = tail * t + term
    tail = tail * t * size * jnp.exp2(x * x * -0.72134752044448)
    return jnp.maximum(x, 0.0) - tail


def dot_nt(a, b):
    return lax.dot_general(a, b, (((1,), (1,)), ((), ())), preferred_element_type=F32)


def kernel(
    n_clu, n_grp, cap, parts,
    tok_hbm, seg_ref, w_in_hbm, b_in_ref, w_out_hbm, b_out_ref, owner_ref, sub_ref,
    pooled_ref, near_ref,
    tok, w_in, w_out, act, member, place, send, send_meta, gath, gath_meta, ret_out, ret_in,
    tok_sem, win_sem, wout_sem, a_send, a_recv, f_send, f_recv, r_send, r_recv,
):
    rows_n, width = tok.shape
    ff = w_in.shape[1]
    docs = pooled_ref.shape[0]
    slots = n_clu * cap
    col = width // parts
    n_y = n_grp // 2
    clu = lax.axis_index("clu")
    grp = lax.axis_index("grp")
    y_at, core = grp // 2, lax.rem(grp, 2)
    sib = y_at * 2 + 1 - core

    def peer(k):
        return lax.rem(clu + k, n_clu)

    def y_peer(t):
        return lax.rem(y_at + t, n_y) * 2 + core

    def y_source(t):
        return lax.rem(y_at + n_y - t, n_y) * 2 + core

    def y_source_sib(t):
        return lax.rem(y_at + n_y - t, n_y) * 2 + 1 - core

    f_parts = win_sem.shape[0]
    f_col = ff // f_parts

    def w_in_copy(f):
        at = pl.ds(pl.multiple_of(f * f_col, f_col), f_col)
        return pltpu.make_async_copy(w_in_hbm.at[:, at], w_in.at[:, at], win_sem.at[f])

    def w_out_copy(q):
        at = pl.ds(q * col, col)
        return pltpu.make_async_copy(w_out_hbm.at[:, at], w_out.at[:, at], wout_sem.at[q])

    tok_copy = pltpu.make_async_copy(tok_hbm, tok, tok_sem)
    tok_copy.start()
    for f in range(f_parts):
        w_in_copy(f).start()
    for q in range(parts):
        w_out_copy(q).start()

    barrier = pltpu.get_barrier_semaphore()
    for k in range(1, n_clu):
        pl.semaphore_signal(barrier, inc=1, device_id=(peer(k), grp), device_id_type=MESH)
    pl.semaphore_signal(barrier, inc=1, device_id=(clu, sib), device_id_type=MESH)
    for t in range(1, n_y):
        pl.semaphore_signal(barrier, inc=1, device_id=(clu, y_peer(t)), device_id_type=MESH)

    member[...] = (
        seg_ref[...] == lax.broadcasted_iota(jnp.int32, (docs, rows_n), 0)
    ).astype(F32).astype(BF16)
    sub = sub_ref[...]
    ones_at = lax.broadcasted_iota(jnp.int32, (docs, docs), 0) == lax.broadcasted_iota(
        jnp.int32, (docs, docs), 1
    )
    owner = owner_ref[...]
    sub_col = jnp.sum(jnp.where(ones_at, sub, 0), axis=1, keepdims=True)
    hits = (lax.broadcasted_iota(jnp.int32, (n_clu, docs), 0) == owner).astype(F32)
    earlier = (
        lax.broadcasted_iota(jnp.int32, (docs, docs), 0)
        < lax.broadcasted_iota(jnp.int32, (docs, docs), 1)
    ).astype(F32).astype(BF16)
    before = jnp.dot(hits.astype(BF16), earlier, preferred_element_type=F32)
    slot = jnp.sum(before * hits, axis=0, keepdims=True).astype(jnp.int32)
    place[...] = (
        lax.broadcasted_iota(jnp.int32, (slots, docs), 0) == owner * cap + slot
    ).astype(F32).astype(BF16)
    lane = lax.broadcasted_iota(jnp.int32, (docs, META), 1)
    code = ((lane == sub_col // LO) | (lane == HI + lax.rem(sub_col, LO))).astype(F32)

    tok_copy.wait()
    blocks = 4
    block = rows_n // blocks

    @pl.loop(0, f_parts)
    def _(f):
        w_in_copy(f).wait()
        at = pl.ds(pl.multiple_of(f * f_col, f_col), f_col)
        bias = b_in_ref[:, at]

        def pre(r):
            return jnp.dot(
                tok[r * block:(r + 1) * block, :], w_in[:, at], preferred_element_type=F32
            )

        now = pre(0)
        for r in range(blocks):
            after = pre(r + 1) if r + 1 < blocks else None
            act[r * block:(r + 1) * block, at] = gelu(now + bias).astype(BF16)
            now = after

    def view(ref, part, g, at):
        return gath_meta.at[g, at] if part == parts else ref.at[g, part, at]

    def a_copy(part, k):
        source = send_meta if part == parts else send.at[part]
        return pltpu.make_async_remote_copy(
            src_ref=source.at[pl.ds(pl.multiple_of(peer(k) * cap, cap), cap)],
            dst_ref=view(gath, part, grp, pl.ds(pl.multiple_of(clu * cap, cap), cap)),
            send_sem=a_send.at[part, k], recv_sem=a_recv.at[part, k],
            device_id=(peer(k), grp), device_id_type=MESH,
        )

    every = pl.ds(0, slots)

    def f_copy(part, which, t):
        if which == "sib":
            g, to, s = grp, sib, 0
        elif which == "y":
            g, to, s = grp, y_peer(t), t
        else:
            g, to, s = y_source(t), sib, n_y - 1 + t
        return pltpu.make_async_remote_copy(
            src_ref=view(gath, part, g, every), dst_ref=view(gath, part, g, every),
            send_sem=f_send.at[part, s], recv_sem=f_recv.at[part, s],
            device_id=(clu, to), device_id_type=MESH,
        )

    def start_a(part, packed):
        source = send_meta if part == parts else send.at[part]
        source[...] = packed.astype(BF16)
        own = pl.ds(pl.multiple_of(clu * cap, cap), cap)
        mine = source[own, :]
        if part == parts:
            gath_meta[grp, own, :] = mine
        else:
            gath[grp, part, own, :] = mine
        for k in range(1, n_clu):
            a_copy(part, k).start()

    def turn(part):
        for k in range(1, n_clu):
            a_copy(part, k).wait_recv()
        for t in range(1, n_y):
            f_copy(part, "y", t).start()
        f_copy(part, "sib", 0).start()

    def pass_on(part):
        for t in range(1, n_y):
            f_copy(part, "y", t).wait_recv()
            f_copy(part, "on", t).start()

    counts = jnp.sum(member[...].astype(F32), axis=1, keepdims=True)
    squares = jnp.zeros((docs, 1), F32)
    for q in range(parts):
        w_out_copy(q).wait()
        at = slice(q * col, (q + 1) * col)
        totals = jnp.zeros((docs, col), F32)
        for r in range(blocks):
            rs = slice(r * block, (r + 1) * block)
            out = jnp.dot(act[rs, :], w_out[:, at], preferred_element_type=F32)
            out = (tok[rs, at].astype(F32) + out + b_out_ref[:, at]).astype(BF16)
            totals += jnp.dot(member[:, rs], out, preferred_element_type=F32)
        mean = totals / counts
        squares += jnp.sum(mean * mean, axis=1, keepdims=True)
        mean16 = mean.astype(BF16)
        pooled_ref[:, at] = mean16
        packed = jnp.dot(place[...], mean16, preferred_element_type=F32)
        if q == 0:
            pl.semaphore_wait(barrier, n_clu - 1 + n_y)
        start_a(q, packed)
        if q >= 2:
            turn(q - 2)
    inv = lax.rsqrt(squares + 1e-06)
    high = inv.astype(BF16).astype(F32)
    middle = (inv - high).astype(BF16).astype(F32)
    low = inv - high - middle
    norm_at = HI + LO
    meta = jnp.where(lane == norm_at, high, code)
    meta = jnp.where(lane == norm_at + 1, middle, meta)
    meta = jnp.where(lane == norm_at + 2, low, meta).astype(BF16)
    start_a(parts, jnp.dot(place[...], meta, preferred_element_type=F32))
    for part in range(max(0, parts - 2), parts + 1):
        turn(part)
    for part in range(parts - 1):
        pass_on(part)

    own_meta = gath_meta[grp]
    meta_lane = lax.broadcasted_iota(jnp.int32, (slots, META), 1)
    is_norm = (meta_lane >= norm_at) & (meta_lane < norm_at + 3)
    own_code = jnp.where(is_norm, 0.0, own_meta.astype(F32)).astype(BF16)
    pick_lane = lax.broadcasted_iota(jnp.int32, (8, META), 1)
    pick = ((pick_lane >= norm_at) & (pick_lane < norm_at + 3)).astype(F32).astype(BF16)
    own_inv = dot_nt(pick, own_meta)

    def best_of(g, itself):
        similar = jnp.zeros((slots, slots), F32)
        for q in range(parts):
            similar += dot_nt(gath[g, q], gath[grp, q])
        g_meta = gath_meta[g]
        inv_g = jnp.sum(jnp.where(is_norm, g_meta.astype(F32), 0.0), axis=1, keepdims=True)
        matched = dot_nt(g_meta, own_code) > 1.5
        if itself:
            matched = matched & (
                lax.broadcasted_iota(jnp.int32, (slots, slots), 0)
                != lax.broadcasted_iota(jnp.int32, (slots, slots), 1)
            )
        values = jnp.where(matched, similar * inv_g * own_inv[0:1, :], -1.0)
        return jnp.max(values, axis=0, keepdims=True)

    best = jnp.maximum(best_of(grp, True), -1.0)
    for part in range(parts + 1):
        f_copy(part, "sib", 0).wait_recv()
    best = jnp.maximum(best, best_of(sib, False))
    for part in range(parts - 1, parts + 1):
        pass_on(part)
    for t in range(1, n_y):
        best = jnp.maximum(best, best_of(y_source(t), False))
    for t in range(1, n_y):
        for part in range(parts + 1):
            f_copy(part, "on", t).wait_recv()
        best = jnp.maximum(best, best_of(y_source_sib(t), False))

    ret_out[...] = jnp.broadcast_to(best, (8, slots))
    ret_in[clu] = jnp.broadcast_to(best, (8, slots))

    def r_copy(k):
        return pltpu.make_async_remote_copy(
            src_ref=ret_out, dst_ref=ret_in.at[clu],
            send_sem=r_send.at[k], recv_sem=r_recv.at[k],
            device_id=(peer(k), grp), device_id_type=MESH,
        )

    for k in range(1, n_clu):
        r_copy(k).start()
    for part in range(parts + 1):
        for k in range(1, n_clu):
            a_copy(part, k).wait_send()
        f_copy(part, "sib", 0).wait_send()
        for t in range(1, n_y):
            f_copy(part, "y", t).wait_send()
            f_copy(part, "on", t).wait_send()
    for k in range(1, n_clu):
        r_copy(k).wait_recv()
    took = (
        lax.broadcasted_iota(jnp.int32, (slots, docs), 0) == clu * cap + slot
    ).astype(F32)
    got = jnp.concatenate([ret_in[c, 0:1, :] for c in range(n_clu)], axis=0)
    spread = jnp.dot(got, took, preferred_element_type=F32, precision=lax.Precision.HIGHEST)
    near_ref[...] = jnp.sum(spread * hits, axis=0, keepdims=True)
    for k in range(1, n_clu):
        r_copy(k).wait_send()


def per_device(tokens, segment_ids, w_in, b_in, w_out, b_out, owner_ids, sub_ids):
    n_clu = lax.axis_size("clu")
    n_grp = lax.axis_size("grp")
    docs = owner_ids.shape[0]
    rows_n, width = tokens.shape
    ff = w_in.shape[1]
    cap = max(16, 2 * docs // n_clu)
    slots = n_clu * cap
    parts = 4
    f_parts = 4
    n_y = n_grp // 2
    vmem = pl.BlockSpec(memory_space=pltpu.VMEM)
    hbm = pl.BlockSpec(memory_space=pl.ANY)
    dma = pltpu.SemaphoreType.DMA
    pooled, near = pl.pallas_call(
        functools.partial(kernel, n_clu, n_grp, cap, parts),
        out_shape=(
            jax.ShapeDtypeStruct((docs, width), BF16),
            jax.ShapeDtypeStruct((1, docs), F32),
        ),
        in_specs=[hbm, vmem, hbm, vmem, hbm, vmem, vmem, vmem],
        out_specs=(vmem, vmem),
        scratch_shapes=[
            pltpu.VMEM((rows_n, width), BF16),
            pltpu.VMEM((width, ff), BF16),
            pltpu.VMEM((ff, width), BF16),
            pltpu.VMEM((rows_n, ff), BF16),
            pltpu.VMEM((docs, rows_n), BF16),
            pltpu.VMEM((slots, docs), BF16),
            pltpu.VMEM((parts, slots, width // parts), BF16),
            pltpu.VMEM((slots, META), BF16),
            pltpu.VMEM((n_grp, parts, slots, width // parts), BF16),
            pltpu.VMEM((n_grp, slots, META), BF16),
            pltpu.VMEM((8, slots), F32),
            pltpu.VMEM((n_clu, 8, slots), F32),
            dma(()),
            dma((f_parts,)),
            dma((parts,)),
            dma((parts + 1, n_clu)),
            dma((parts + 1, n_clu)),
            dma((parts + 1, 2 * n_y)),
            dma((parts + 1, 2 * n_y)),
            dma((n_clu,)),
            dma((n_clu,)),
        ],
        compiler_params=pltpu.CompilerParams(
            collective_id=0, has_side_effects=True, vmem_limit_bytes=56 * 1024 * 1024
        ),
    )(
        tokens, segment_ids, w_in, b_in.reshape(1, ff), w_out, b_out.reshape(1, width),
        owner_ids.reshape(1, docs), sub_ids.reshape(1, docs),
    )
    return (pooled, near.reshape(docs))


def solution(mesh):
    in_specs = (
        P(("clu", "grp"), None),
        P(("clu", "grp"), None),
        P(),
        P(),
        P(),
        P(),
        P(("clu", "grp"), None),
        P(("clu", "grp")),
    )
    out_specs = (P(("clu", "grp"), None), P(("clu", "grp")))
    return jax.shard_map(
        per_device, mesh=mesh, in_specs=in_specs, out_specs=out_specs, check_vma=False
    )
```
